256 devices in a mesh: blk: 32 (over x, z_lo, core), tensor: 8 (over z_hi, y).
Axes of the slice: x: 4, y: 4, z: 8 (z_hi: 2, z_lo: 4; z = z_hi * 4 + z_lo), core: 2. Of those that a mesh axis runs over, the one named last changes fastest.
Arguments:
- queries: bfloat16 [2048, 4096], P('blk', 'tensor'), may hold values from -64 to 64
- prefix_keys: bfloat16 [32768, 1024], P('blk', 'tensor'), may hold values from -6 to 6
- prefix_values: bfloat16 [32768, 1024], P('blk', 'tensor'), may hold values from -6 to 6
- suffix_keys: bfloat16 [2048, 128, 1024], P('blk', None, 'tensor'), may hold values from -16 to 16
- suffix_values: bfloat16 [2048, 128, 1024], P('blk', None, 'tensor'), may hold values from -6 to 6
- suffix_lengths: int32 [2048], P('blk'), may hold values from 32 to 128, as said below
- out_weight: bfloat16 [4096, 8192], P('tensor'), may hold values from -0.09375 to 0.09375
Outputs:
- attended: bfloat16 [2048, 8192], P('blk', 'tensor')
The draws below stay inside these ranges and needn't reach their ends.
Inputs may be any that keep to these rules, and one draw needn't show every extreme that they name: `suffix_lengths`: some completion has exactly 128 live suffix slots.
All inputs are finite; a program needn't handle non-finite values.
Results may differ from the reference program's by a relative error of at most 0.01555.
Values may be sent and summed in bfloat16 or wider, within the bound.
No kernel may reach another device: no remote copies, remote signals or barrier semaphores. Data moves between devices by JAX's collectives and lax.ppermute only.
A program may use at most 128 MiB of HBM per device.

```python
import math
import jax
import jax.numpy as jnp
from jax import lax

D = 8192
KVH = 8
DH = 128
QH = 32
ROWS_DEV = 64
P_DEV = 1024
S_MAX = 128
COMPL = 2048
PREFIX = 32768


def shared_fields(key):
    key_query, key_prompt = jax.random.split(key)
    query_all = jnp.clip(jax.random.normal(key_query, (COMPL, QH * DH), jnp.float32) * 2.0, -8.0, 8.0)
    prompt_keys = jnp.clip(jax.random.normal(key_prompt, (PREFIX, KVH * DH), jnp.float32) * 1.5, -6.0, 6.0)
    return (query_all, prompt_keys)


def draw_queries(key, part):
    query_all, prompt_keys = shared_fields(key)
    return jnp.clip(query_all, -64.0, 64.0).astype(jnp.bfloat16)


def draw_prefix_keys(key, part):
    query_all, prompt_keys = shared_fields(key)
    return prompt_keys.astype(jnp.bfloat16)


def draw_suffix_lengths(key, part):
    key = jax.random.fold_in(key, 23)
    key_cap, key_len, key_pick, key_row = jax.random.split(key, 4)
    device_count = COMPL // ROWS_DEV
    caps = jax.random.randint(key_cap, (device_count,), S_MAX // 2, S_MAX + 1)
    pick = jax.random.randint(key_pick, (), 0, device_count)
    caps = jnp.where(jnp.arange(device_count, dtype=jnp.int32) == pick, S_MAX, caps)
    row_caps = jnp.repeat(caps, ROWS_DEV)
    floors = row_caps // 2
    raw = jax.random.randint(key_len, (COMPL,), 0, 1 << 20)
    lengths = floors + raw % (row_caps - floors + 1)
    full_row = pick * ROWS_DEV + jax.random.randint(key_row, (), 0, ROWS_DEV)
    lengths = jnp.where(jnp.arange(COMPL, dtype=jnp.int32) == full_row, S_MAX, lengths)
    return lengths.astype(jnp.int32)


def block_scale(key, dims, cuts, low, top_value):
    def one(position, shards_of):
        heights = jax.random.uniform(jax.random.fold_in(jax.random.fold_in(key, 6), position), (shards_of,), jnp.float32, low / len(cuts), top_value / len(cuts))
        return jnp.repeat(jnp.exp(heights), dims[position] // shards_of).reshape((-1,) + (1,) * (len(dims) - position - 1))

    factor_of = one(*cuts[0])
    for cut in cuts[1:]:
        factor_of = factor_of * one(*cut)
    return factor_of


def bell_draw(rng, shape, deviation, limit, cuts=(), kind=jnp.bfloat16):
    entries = jax.random.normal(rng, shape, jnp.float32) * deviation
    if len(cuts) > 0:
        entries = block_scale(rng, shape, cuts, -0.22, 0.18) * entries
    return jnp.clip(entries, min=-limit, max=limit).astype(kind)


def setup_inputs(seed: int = 0) -> dict:
    seeds = jax.random.split(jax.random.key(seed), 8)
    return {
        "queries": draw_queries(jax.random.fold_in(seeds[7], 71), 0),
        "prefix_keys": draw_prefix_keys(jax.random.fold_in(seeds[7], 71), 0),
        "prefix_values": bell_draw(seeds[2], (PREFIX, KVH * DH), 1.0, 6.0, ((0, 32), (1, 8))),
        "suffix_keys": bell_draw(seeds[3], (COMPL, S_MAX, KVH * DH), 2.5, 16.0, ((0, 32), (2, 8))),
        "suffix_values": bell_draw(seeds[4], (COMPL, S_MAX, KVH * DH), 1.0, 6.0, ((0, 32), (2, 8))),
        "suffix_lengths": draw_suffix_lengths(jax.random.fold_in(seeds[7], 71), 0),
        "out_weight": bell_draw(seeds[6], (QH * DH, D), (QH * DH) ** -0.5, 0.09375, ((0, 8),)),
    }


def merge_pair(carry, part):
    peak_a, total_a, mixed_a = carry
    peak_b, total_b, mixed_b = part
    peak_new = jnp.maximum(peak_a, peak_b)
    factor_a = jnp.exp(peak_a - peak_new)
    factor_b = jnp.exp(peak_b - peak_new)
    return (peak_new, total_a * factor_a + total_b * factor_b, mixed_a * factor_a[..., None] + mixed_b * factor_b[..., None])

def block_partial(query_head, key_block, value_block, score_scale):
    scores = jnp.einsum('cgd,pd->cgp', query_head, key_block.astype(jnp.float32)) * score_scale
    peaks = lax.optimization_barrier(jnp.max(scores, axis=-1))
    weights = jnp.exp(scores - peaks[..., None])
    totals = lax.optimization_barrier(jnp.sum(weights, axis=-1))
    rounded = lax.optimization_barrier(weights.astype(jnp.bfloat16)).astype(jnp.float32)
    mixed = jnp.einsum('cgp,pd->cgd', rounded, value_block.astype(jnp.float32))
    return (peaks, totals, mixed)

def reference(queries, prefix_keys, prefix_values, suffix_keys, suffix_values, suffix_lengths, out_weight):
    group = QH // KVH
    score_scale = 1.0 / math.sqrt(DH)
    query_all = queries.astype(jnp.float32).reshape(COMPL, KVH, group, DH)
    key_all = prefix_keys.reshape(PREFIX, KVH, DH)
    value_all = prefix_values.reshape(PREFIX, KVH, DH)
    suffix_key_all = suffix_keys.reshape(COMPL, S_MAX, KVH, DH)
    suffix_value_all = suffix_values.reshape(COMPL, S_MAX, KVH, DH)
    positions = jnp.arange(S_MAX, dtype=jnp.int32)
    live = positions[None, None, :] < suffix_lengths.astype(jnp.int32)[:, None, None]

    def one_head(head):
        query_head = query_all[:, head]
        suffix_key = suffix_key_all[:, :, head].astype(jnp.float32)
        suffix_value = suffix_value_all[:, :, head].astype(jnp.float32)
        scores = jnp.einsum('cgd,csd->cgs', query_head, suffix_key) * score_scale
        peaks = lax.optimization_barrier(jnp.max(jnp.where(live, scores, -jnp.inf), axis=-1))
        weights = jnp.where(live, jnp.exp(scores - peaks[..., None]), jnp.zeros_like(scores))
        totals = lax.optimization_barrier(jnp.sum(weights, axis=-1))
        rounded = lax.optimization_barrier(weights.astype(jnp.bfloat16)).astype(jnp.float32)
        mixed = jnp.einsum('cgs,csd->cgd', rounded, suffix_value)
        key_blocks = key_all[:, head].reshape(PREFIX // P_DEV, P_DEV, DH)
        value_blocks = value_all[:, head].reshape(PREFIX // P_DEV, P_DEV, DH)

        def step_block(carry, blocks):
            return (merge_pair(carry, block_partial(query_head, blocks[0], blocks[1], score_scale)), None)
        final, _ = lax.scan(step_block, (peaks, totals, mixed), (key_blocks, value_blocks))
        return final[2] / final[1][..., None]
    heads_out = lax.map(one_head, jnp.arange(KVH, dtype=jnp.int32))
    attention = jnp.transpose(heads_out, (1, 0, 2, 3)).reshape(COMPL, QH * DH).astype(jnp.bfloat16)
    return jnp.dot(attention, out_weight, preferred_element_type=jnp.float32).astype(jnp.bfloat16)
```

```python
import functools
import math

import jax
import jax.numpy as jnp
from jax import lax
from jax.experimental import pallas as pl
from jax.experimental.pallas import tpu as pltpu
from jax.sharding import PartitionSpec as P

DH = 128
GROUP = 4
WIDTH = GROUP * DH
LOG2E = math.log2(math.e)
SCALE2 = LOG2E / math.sqrt(DH)
F32 = jnp.float32
BF16 = jnp.bfloat16
VMEM_LIMIT = 56 << 20

NX, NZ, NC = 4, 4, 2
NH, NY = 2, 4


def blk_perm(dx=0, dz=0, dc=0):
    pairs = []
    for x in range(NX):
        for z in range(NZ):
            for c in range(NC):
                there = ((x + dx) % NX * NZ + (z + dz) % NZ) * NC + (c + dc) % NC
                pairs.append(((x * NZ + z) * NC + c, there))
    return pairs


def tensor_perm(dh=0, dy=0):
    return [
        (h * NY + y, (h + dh) % NH * NY + (y + dy) % NY) for h in range(NH) for y in range(NY)
    ]


def params():
    return pltpu.CompilerParams(vmem_limit_bytes=VMEM_LIMIT)


def cost(flops, nbytes, transcendentals=0):
    return pl.CostEstimate(flops=flops, bytes_accessed=nbytes, transcendentals=transcendentals)


def heads_of(q):
    return jnp.concatenate([q[:, h * DH : (h + 1) * DH] for h in range(GROUP)], axis=0)


SUB = 16


def suffix_kernel(len_ref, q_ref, k_ref, v_ref, o_ref, lse_ref):
    slots = k_ref.shape[1]
    first = pl.program_id(0) * SUB
    q = heads_of(q_ref[...])
    k = k_ref[...].reshape(SUB * slots, DH)
    v = v_ref[...].reshape(SUB * slots, DH)
    s = lax.dot_general(q, k, (((1,), (1,)), ((), ())), preferred_element_type=F32)
    row = lax.broadcasted_iota(jnp.int32, (SUB, slots), 0)
    col = lax.broadcasted_iota(jnp.int32, (SUB, slots), 1)
    tiles = [(row == j) & (col < len_ref[first + j]) for j in range(SUB)]
    live = jnp.concatenate(tiles, axis=1)
    live = jnp.concatenate([live] * GROUP, axis=0)
    s = jnp.where(live, s * SCALE2, -jnp.inf)
    peak = jnp.max(s, axis=1, keepdims=True)
    p = jnp.exp2(s - peak)
    total = jnp.sum(p, axis=1, keepdims=True)
    mixed = jnp.dot(p.astype(BF16), v, preferred_element_type=F32) / total
    lse = peak + jnp.log2(total)
    lane = lax.broadcasted_iota(jnp.int32, (SUB, DH), 1)
    stat = jnp.zeros((SUB, DH), F32)
    for h in range(GROUP):
        o_ref[:, h * DH : (h + 1) * DH] = mixed[h * SUB : (h + 1) * SUB]
        stat = jnp.where(lane == h, lse[h * SUB : (h + 1) * SUB], stat)
    lse_ref[...] = stat


def suffix_partial(q, sk, sv, lengths):
    rows, slots, _ = sk.shape
    return pl.pallas_call(
        suffix_kernel,
        grid_spec=pltpu.PrefetchScalarGridSpec(
            num_scalar_prefetch=1,
            grid=(rows // SUB,),
            in_specs=[
                pl.BlockSpec((SUB, WIDTH), lambda i, _: (i, 0)),
                pl.BlockSpec((SUB, slots, DH), lambda i, _: (i, 0, 0)),
                pl.BlockSpec((SUB, slots, DH), lambda i, _: (i, 0, 0)),
            ],
            out_specs=[
                pl.BlockSpec((SUB, WIDTH), lambda i, _: (i, 0)),
                pl.BlockSpec((SUB, DH), lambda i, _: (i, 0)),
            ],
        ),
        out_shape=[
            jax.ShapeDtypeStruct((rows, WIDTH), F32),
            jax.ShapeDtypeStruct((rows, DH), F32),
        ],
        compiler_params=params(),
        cost_estimate=cost(4 * rows * WIDTH * slots * SUB, 4 * rows * slots * DH),
    )(lengths, q, sk, sv)


def prefix_kernel(groups, blocks, first, last, *refs):
    refs = list(refs)
    qs = [refs.pop(0) for _ in range(groups)]
    kvs = []
    for kind in blocks:
        if kind == "pair":
            kvs.append((refs.pop(0), 0, refs.pop(0), 0))
        else:
            both = refs.pop(0)
            kvs.append((both, 0, both, both.shape[0] // 2))
    if not first:
        acc_in, stat_in = refs.pop(0), refs.pop(0)
    rows = qs[0].shape[0]
    total_rows = GROUP * rows
    lane = lax.broadcasted_iota(jnp.int32, (total_rows, DH), 1)
    for g in range(groups):
        q = heads_of(qs[g][...])
        span = slice(g * total_rows, (g + 1) * total_rows)
        peak = None
        if not first:
            acc = acc_in[span, :]
            peak = stat_in[span, 0:1]
            total = stat_in[span, DH // 2 : DH // 2 + 1]
        for k_ref, k_at, v_ref, v_at in kvs:
            size = v_ref.shape[0] - v_at
            k = k_ref[k_at : k_at + size, :]
            v = v_ref[v_at : v_at + size, :]
            s = lax.dot_general(q, k, (((1,), (1,)), ((), ())), preferred_element_type=F32)
            top = jnp.max(s, axis=1, keepdims=True) * SCALE2
            new = top if peak is None else jnp.maximum(peak, top)
            p = jnp.exp2(s * SCALE2 - new).astype(BF16)
            both = jnp.dot(
                p,
                jnp.concatenate([v, jnp.ones_like(v)], axis=1),
                preferred_element_type=F32,
            )
            if peak is None:
                acc, total = both[:, :DH], both[:, DH : DH + 1]
            else:
                fade = jnp.exp2(peak - new)
                acc = acc * fade + both[:, :DH]
                total = total * fade + both[:, DH : DH + 1]
            peak = new
        if last:
            o_ref = refs[g]
            mixed = (acc / total).astype(BF16)
            lse = peak + jnp.log2(total)
            stat = jnp.zeros((rows, DH), F32)
            for h in range(GROUP):
                part = slice(h * rows, (h + 1) * rows)
                o_ref[:, h * DH : (h + 1) * DH] = mixed[part]
                rest = lse[part]
                for j in range(3):
                    piece = rest.astype(BF16).astype(F32)
                    rest = rest - piece
                    stat = jnp.where(lane[:rows] == 3 * h + j, piece, stat)
            o_ref[:, WIDTH:] = stat.astype(BF16)
        else:
            refs[0][span, :] = acc
            refs[1][span, :] = jnp.where(lane < DH // 2, peak, total)


def prefix_partial(queries, blocks, state, last):
    rows = queries[0].shape[0]
    groups = len(queries)
    all_rows = groups * GROUP * rows
    kinds, arrays, keys = [], [], 0
    for block in blocks:
        if isinstance(block, tuple):
            kinds.append("pair")
            arrays += list(block)
            keys += block[0].shape[0]
        else:
            kinds.append("both")
            arrays.append(block)
            keys += block.shape[0] // 2
    if last:
        outs = [jax.ShapeDtypeStruct((rows, WIDTH + DH), BF16)] * groups
    else:
        outs = [jax.ShapeDtypeStruct((all_rows, DH), F32)] * 2
    return pl.pallas_call(
        functools.partial(prefix_kernel, groups, tuple(kinds), state is None, last),
        out_shape=outs,
        compiler_params=params(),
        cost_estimate=cost(8 * all_rows * DH * keys, 4 * keys * DH, all_rows * keys),
    )(*queries, *arrays, *(state or ()))


def merged(parts, mixed, lse):
    columns = []
    for h in range(GROUP):
        span = slice(h * DH, (h + 1) * DH)
        logs, values = [lse[:, h : h + 1]], [mixed[:, span]]
        for part in parts:
            stat = part[:, WIDTH:].astype(F32)
            at = 3 * h
            logs.append(stat[:, at : at + 1] + stat[:, at + 1 : at + 2] + stat[:, at + 2 : at + 3])
            values.append(part[:, span].astype(F32))
        peak = functools.reduce(jnp.maximum, logs)
        weights = [jnp.exp2(log - peak) for log in logs]
        total = functools.reduce(jnp.add, weights)
        value = functools.reduce(jnp.add, [w * o for w, o in zip(weights, values)])
        columns.append((value / total).astype(BF16))
    return jnp.concatenate(columns, axis=1)


def project_kernel(n_parts, merge, index_ref, *refs):
    refs = list(refs)
    if merge:
        parts = [refs.pop(0) for _ in range(n_parts)]
        mixed, lse = refs.pop(0), refs.pop(0)
        weights, refs = refs[:NY], refs[NY:]
        outs, att_ref = refs[:NY], refs[NY]

        @pl.when(pl.program_id(0) == 0)
        def _():
            att_ref[...] = merged([p[...] for p in parts], mixed[...], lse[...])
    else:
        att_ref = refs.pop(0)
        weights, outs = refs[:NY], refs[NY:]
    att = att_ref[...]
    for w, o in zip(weights, outs):
        o[...] = jnp.dot(att, w[...], preferred_element_type=F32).astype(o.dtype)


STEPS = 4


def project(index, inputs, weight, merge):
    rows = inputs[0].shape[0]
    depth, columns = weight.shape
    piece = columns // (NH * NY)
    tile = piece // STEPS

    def whole(a):
        return pl.BlockSpec(a.shape, lambda i, _: (0, 0))

    def block(k):
        return pl.BlockSpec((depth, tile), lambda i, at: (0, at[k] * STEPS + i))

    out_shape = [jax.ShapeDtypeStruct((rows, piece), F32 if k == 0 else BF16) for k in range(NY)]
    out_specs = [pl.BlockSpec((rows, tile), lambda i, _: (0, i)) for _ in range(NY)]
    if merge:
        out_shape.append(jax.ShapeDtypeStruct((rows, depth), BF16))
        out_specs.append(pl.BlockSpec((rows, depth), lambda i, _: (0, 0)))
    return pl.pallas_call(
        functools.partial(project_kernel, len(inputs) - 2, merge),
        grid_spec=pltpu.PrefetchScalarGridSpec(
            num_scalar_prefetch=1,
            grid=(STEPS,),
            in_specs=[whole(a) for a in inputs] + [block(k) for k in range(NY)],
            out_specs=out_specs,
        ),
        out_shape=out_shape,
        compiler_params=params(),
        cost_estimate=cost(2 * rows * depth * piece * NY, 2 * depth * piece * NY),
    )(index, *inputs, *([weight] * NY))


def on_device(
    queries, prefix_keys, prefix_values, suffix_keys, suffix_values, suffix_lengths, out_weight
):
    send = functools.partial(lax.ppermute, axis_name="blk")
    both = jnp.concatenate([prefix_keys, prefix_values], axis=0)
    peer = send(both, perm=blk_perm(dc=1))
    near = [send(both, perm=blk_perm(dx=d)) for d in (1, 3)]
    far = send(both, perm=blk_perm(dx=2))
    group = [queries] + [send(queries, perm=blk_perm(dz=d)) for d in (1, 2, 3)]

    mixed, lse = suffix_partial(queries, suffix_keys, suffix_values, suffix_lengths)

    state = prefix_partial(group, [(prefix_keys, prefix_values), peer], None, False)
    near_peer = [send(b, perm=blk_perm(dc=1)) for b in near]
    state = prefix_partial(group, near, state, False)
    far_peer = send(far, perm=blk_perm(dc=1))
    parts = prefix_partial(group, near_peer + [far, far_peer], state, True)
    parts = [parts[0]] + [send(parts[d], perm=blk_perm(dz=-d)) for d in (1, 2, 3)]

    here = lax.axis_index("tensor")
    half, line = here // NY, here % NY
    lines = (line + jnp.arange(NY, dtype=jnp.int32)) % NY
    send = functools.partial(lax.ppermute, axis_name="tensor")
    *away, attention = project((NH - 1 - half) * NY + lines, parts + [mixed, lse], out_weight, True)
    away = [away[0]] + [send(away[d], perm=tensor_perm(dy=d)) for d in (1, 2, 3)]
    home = project(half * NY + lines, [attention], out_weight, False)
    home = [home[0]] + [send(home[d], perm=tensor_perm(dy=d)) for d in (1, 2, 3)]

    def summed(pieces):
        return functools.reduce(jnp.add, [p.astype(F32) for p in pieces])

    other = send(summed(away).astype(BF16), perm=tensor_perm(dh=1))
    return summed(home + [other]).astype(BF16)


def solution(mesh):
    in_specs = (
        P("blk", "tensor"),
        P("blk", "tensor"),
        P("blk", "tensor"),
        P("blk", None, "tensor"),
        P("blk", None, "tensor"),
        P("blk"),
        P("tensor", None),
    )
    out_specs = P("blk", "tensor")
    return jax.shard_map(
        on_device, mesh=mesh, in_specs=in_specs, out_specs=out_specs, check_vma=False
    )
```

```python
import functools
import math

import jax
import jax.numpy as jnp
from jax import lax
from jax.experimental import pallas as pl
from jax.experimental.pallas import tpu as pltpu
from jax.sharding import PartitionSpec as P

DH = 128
GROUP = 4
WIDTH = GROUP * DH
LOG2E = math.log2(math.e)
SCALE2 = LOG2E / math.sqrt(DH)
F32 = jnp.float32
BF16 = jnp.bfloat16

NX, NZ, NC = 4, 4, 2
NH, NY = 2, 4


def blk_perm(dx=0, dz=0, dc=0):
    pairs = []
    for x in range(NX):
        for z in range(NZ):
            for c in range(NC):
                there = ((x + dx) % NX * NZ + (z + dz) % NZ) * NC + (c + dc) % NC
                pairs.append(((x * NZ + z) * NC + c, there))
    return pairs


def tensor_perm(dh=0, dy=0):
    return [
        (h * NY + y, (h + dh) % NH * NY + (y + dy) % NY) for h in range(NH) for y in range(NY)
    ]


def params(mib):
    return pltpu.CompilerParams(vmem_limit_bytes=mib << 20)


def cost(micros):
    return pl.CostEstimate(flops=int(micros * 1.1e9), bytes_accessed=1 << 20, transcendentals=0)


def heads_of(q):
    return jnp.concatenate([q[:, h * DH : (h + 1) * DH] for h in range(GROUP)], axis=0)


SUB = 16


def suffix_kernel(len_ref, q_ref, k_ref, v_ref, o_ref, lse_ref):
    slots = k_ref.shape[1]
    first = pl.program_id(0) * SUB
    q = heads_of(q_ref[...])
    k = k_ref[...].reshape(SUB * slots, DH)
    v = v_ref[...].reshape(SUB * slots, DH)
    s = lax.dot_general(q, k, (((1,), (1,)), ((), ())), preferred_element_type=F32)
    row = lax.broadcasted_iota(jnp.int32, (SUB, slots), 0)
    col = lax.broadcasted_iota(jnp.int32, (SUB, slots), 1)
    tiles = [(row == j) & (col < len_ref[first + j]) for j in range(SUB)]
    live = jnp.concatenate(tiles, axis=1)
    live = jnp.concatenate([live] * GROUP, axis=0)
    s = jnp.where(live, s * SCALE2, -jnp.inf)
    peak = jnp.max(s, axis=1, keepdims=True)
    p = jnp.exp2(s - peak)
    total = jnp.sum(p, axis=1, keepdims=True)
    mixed = jnp.dot(p.astype(BF16), v, preferred_element_type=F32) / total
    lse = peak + jnp.log2(total)
    lane = lax.broadcasted_iota(jnp.int32, (SUB, DH), 1)
    stat = jnp.zeros((SUB, DH), F32)
    for h in range(GROUP):
        o_ref[:, h * DH : (h + 1) * DH] = mixed[h * SUB : (h + 1) * SUB]
        stat = jnp.where(lane == h, lse[h * SUB : (h + 1) * SUB], stat)
    lse_ref[...] = stat


def suffix_partial(q, sk, sv, lengths):
    rows, slots, _ = sk.shape
    return pl.pallas_call(
        suffix_kernel,
        grid_spec=pltpu.PrefetchScalarGridSpec(
            num_scalar_prefetch=1,
            grid=(rows // SUB,),
            in_specs=[
                pl.BlockSpec((SUB, WIDTH), lambda i, _: (i, 0)),
                pl.BlockSpec((SUB, slots, DH), lambda i, _: (i, 0, 0)),
                pl.BlockSpec((SUB, slots, DH), lambda i, _: (i, 0, 0)),
            ],
            out_specs=[
                pl.BlockSpec((SUB, WIDTH), lambda i, _: (i, 0)),
                pl.BlockSpec((SUB, DH), lambda i, _: (i, 0)),
            ],
        ),
        out_shape=[
            jax.ShapeDtypeStruct((rows, WIDTH), F32),
            jax.ShapeDtypeStruct((rows, DH), F32),
        ],
        compiler_params=params(12),
        cost_estimate=cost(3.0),
    )(lengths, q, sk, sv)


def stack_kernel(a_ref, b_ref, o_ref, sems):
    rows = a_ref.shape[0]
    copies = [
        pltpu.make_async_copy(ref, o_ref.at[pl.ds(i * rows, rows)], sems.at[i])
        for i, ref in enumerate((a_ref, b_ref))
    ]
    for copy in copies:
        copy.start()
    for copy in copies:
        copy.wait()


def stacked(a, b):
    rows, width = a.shape
    return pl.pallas_call(
        stack_kernel,
        in_specs=[pl.BlockSpec(memory_space=pl.ANY)] * 2,
        out_specs=pl.BlockSpec(memory_space=pltpu.VMEM),
        out_shape=jax.ShapeDtypeStruct((2 * rows, width), a.dtype),
        scratch_shapes=[pltpu.SemaphoreType.DMA((2,))],
        compiler_params=params(4),
        cost_estimate=cost(0.8),
    )(a, b)


def prefix_kernel(groups, blocks, first, last, *refs):
    refs = list(refs)
    qs = [refs.pop(0) for _ in range(groups)]
    kvs = []
    for kind in blocks:
        if kind == "pair":
            kvs.append((refs.pop(0), 0, refs.pop(0), 0))
        else:
            both = refs.pop(0)
            kvs.append((both, 0, both, both.shape[0] // 2))
    if not first:
        acc_in, stat_in = refs.pop(0), refs.pop(0)
    rows = qs[0].shape[0]
    total_rows = GROUP * rows
    lane = lax.broadcasted_iota(jnp.int32, (total_rows, DH), 1)
    for g in range(groups):
        q = heads_of(qs[g][...])
        span = slice(g * total_rows, (g + 1) * total_rows)
        peak = None
        if not first:
            acc = acc_in[span, :]
            peak = stat_in[span, 0:1]
            total = stat_in[span, DH // 2 : DH // 2 + 1]
        for k_ref, k_at, v_ref, v_at in kvs:
            size = v_ref.shape[0] - v_at
            k = k_ref[k_at : k_at + size, :]
            v = v_ref[v_at : v_at + size, :]
            s = lax.dot_general(q, k, (((1,), (1,)), ((), ())), preferred_element_type=F32)
            top = jnp.max(s, axis=1, keepdims=True) * SCALE2
            new = top if peak is None else jnp.maximum(peak, top)
            p = jnp.exp2(s * SCALE2 - new).astype(BF16)
            both = jnp.dot(
                p,
                jnp.concatenate([v, jnp.ones_like(v)], axis=1),
                preferred_element_type=F32,
            )
            if peak is None:
                acc, total = both[:, :DH], both[:, DH : DH + 1]
            else:
                fade = jnp.exp2(peak - new)
                acc = acc * fade + both[:, :DH]
                total = total * fade + both[:, DH : DH + 1]
            peak = new
        if last:
            o_ref = refs[g]
            mixed = (acc / total).astype(BF16)
            lse = peak + jnp.log2(total)
            stat = jnp.zeros((rows, DH), F32)
            for h in range(GROUP):
                part = slice(h * rows, (h + 1) * rows)
                o_ref[:, h * DH : (h + 1) * DH] = mixed[part]
                rest = lse[part]
                for j in range(3):
                    piece = rest.astype(BF16).astype(F32)
                    rest = rest - piece
                    stat = jnp.where(lane[:rows] == 3 * h + j, piece, stat)
            o_ref[:, WIDTH:] = stat.astype(BF16)
        else:
            refs[0][span, :] = acc
            refs[1][span, :] = jnp.where(lane < DH // 2, peak, total)


def prefix_partial(queries, blocks, state, last):
    rows = queries[0].shape[0]
    groups = len(queries)
    all_rows = groups * GROUP * rows
    kinds, arrays, keys = [], [], 0
    for block in blocks:
        if isinstance(block, tuple):
            kinds.append("pair")
            arrays += list(block)
            keys += block[0].shape[0]
        else:
            kinds.append("both")
            arrays.append(block)
            keys += block.shape[0] // 2
    if last:
        outs = [jax.ShapeDtypeStruct((rows, WIDTH + DH), BF16)] * groups
    else:
        outs = [jax.ShapeDtypeStruct((all_rows, DH), F32)] * 2
    return pl.pallas_call(
        functools.partial(prefix_kernel, groups, tuple(kinds), state is None, last),
        out_shape=outs,
        compiler_params=params(16),
        cost_estimate=cost(0.5 + 1.4e-6 * all_rows * keys),
    )(*queries, *arrays, *(state or ()))


def merged(parts, mixed, lse):
    columns = []
    for h in range(GROUP):
        span = slice(h * DH, (h + 1) * DH)
        logs, values = [lse[:, h : h + 1]], [mixed[:, span]]
        for part in parts:
            stat = part[:, WIDTH:].astype(F32)
            at = 3 * h
            logs.append(stat[:, at : at + 1] + stat[:, at + 1 : at + 2] + stat[:, at + 2 : at + 3])
            values.append(part[:, span].astype(F32))
        peak = functools.reduce(jnp.maximum, logs)
        weights = [jnp.exp2(log - peak) for log in logs]
        total = functools.reduce(jnp.add, weights)
        value = functools.reduce(jnp.add, [w * o for w, o in zip(weights, values)])
        columns.append((value / total).astype(BF16))
    return jnp.concatenate(columns, axis=1)


def project_kernel(n_parts, merge, index_ref, *refs):
    refs = list(refs)
    if merge:
        parts = [refs.pop(0) for _ in range(n_parts)]
        mixed, lse = refs.pop(0), refs.pop(0)
        weights, refs = refs[:NY], refs[NY:]
        outs, att_ref = refs[:NY], refs[NY]

        @pl.when(pl.program_id(0) == 0)
        def _():
            att_ref[...] = merged([p[...] for p in parts], mixed[...], lse[...])
    else:
        att_ref = refs.pop(0)
        weights, outs = refs[:NY], refs[NY:]
    att = att_ref[...]
    for w, o in zip(weights, outs):
        o[...] = jnp.dot(att, w[...], preferred_element_type=F32).astype(o.dtype)


STEPS = 4


def project(index, first, inputs, weight, merge):
    rows = inputs[0].shape[0]
    depth, columns = weight.shape
    piece = columns // (NH * NY)
    tile = piece // STEPS

    def whole(a):
        return pl.BlockSpec(a.shape, lambda i, _: (0, 0))

    def block(k):
        return pl.BlockSpec((depth, tile), lambda i, at: (0, at[first + k] * STEPS + i))

    out_shape = [jax.ShapeDtypeStruct((rows, piece), F32 if k == 0 else BF16) for k in range(NY)]
    out_specs = [pl.BlockSpec((rows, tile), lambda i, _: (0, i)) for _ in range(NY)]
    if merge:
        out_shape.append(jax.ShapeDtypeStruct((rows, depth), BF16))
        out_specs.append(pl.BlockSpec((rows, depth), lambda i, _: (0, 0)))
    return pl.pallas_call(
        functools.partial(project_kernel, len(inputs) - 2, merge),
        grid_spec=pltpu.PrefetchScalarGridSpec(
            num_scalar_prefetch=1,
            grid=(STEPS,),
            in_specs=[whole(a) for a in inputs] + [block(k) for k in range(NY)],
            out_specs=out_specs,
        ),
        out_shape=out_shape,
        compiler_params=params(12),
        cost_estimate=cost(3.0),
    )(index, *inputs, *([weight] * NY))


def on_device(
    queries, prefix_keys, prefix_values, suffix_keys, suffix_values, suffix_lengths, out_weight
):
    here = lax.axis_index("tensor").astype(jnp.int32)
    step = jnp.arange(NH * NY, dtype=jnp.int32)
    index = (here + NY * (1 - step // NY)) // NY % NH * NY + (here + step) % NY

    send = functools.partial(lax.ppermute, axis_name="blk")
    group = [queries] + [send(queries, perm=blk_perm(dz=d)) for d in (1, 2, 3)]
    both = stacked(prefix_keys, prefix_values)
    near = [send(both, perm=blk_perm(dx=d)) for d in (1, 3)]
    peer = send(both, perm=blk_perm(dc=1))
    far = send(both, perm=blk_perm(dx=2))

    together = lax.optimization_barrier
    mixed, lse = suffix_partial(queries, suffix_keys, suffix_values, suffix_lengths)
    peer, lse, index = together((peer, lse, index))
    state = prefix_partial(group, [(prefix_keys, prefix_values), peer], None, False)
    near, state = together((near, state))
    near_peer = [send(b, perm=blk_perm(dc=1)) for b in near]
    state = prefix_partial(group, near, state, False)
    far, state = together((far, state))
    far_peer = send(far, perm=blk_perm(dc=1))
    state = prefix_partial(group, near_peer, state, False)
    far_peer, state = together((far_peer, state))
    parts = prefix_partial(group, [far, far_peer], state, True)
    parts = [parts[0]] + [send(parts[d], perm=blk_perm(dz=-d)) for d in (1, 2, 3)]

    send = functools.partial(lax.ppermute, axis_name="tensor")
    *away, attention = project(index, 0, parts + [mixed, lse], out_weight, True)
    away = [away[0]] + [send(away[d], perm=tensor_perm(dy=d)) for d in (1, 2, 3)]
    home = project(index, NY, [attention], out_weight, False)
    home = [home[0]] + [send(home[d], perm=tensor_perm(dy=d)) for d in (1, 2, 3)]

    def summed(pieces):
        return functools.reduce(jnp.add, [p.astype(F32) for p in pieces])

    other = send(summed(away).astype(BF16), perm=tensor_perm(dh=1))
    return summed(home + [other]).astype(BF16)


def solution(mesh):
    in_specs = (
        P("blk", "tensor"),
        P("blk", "tensor"),
        P("blk", "tensor"),
        P("blk", None, "tensor"),
        P("blk", None, "tensor"),
        P("blk"),
        P("tensor", None),
    )
    out_specs = P("blk", "tensor")
    return jax.shard_map(
        on_device, mesh=mesh, in_specs=in_specs, out_specs=out_specs, check_vma=False
    )
```

```python
import functools
import math

import jax
import jax.numpy as jnp
from jax import lax
from jax.experimental import pallas as pl
from jax.experimental.pallas import tpu as pltpu
from jax.sharding import PartitionSpec as P

DH = 128
GROUP = 4
WIDTH = GROUP * DH
LOG2E = math.log2(math.e)
SCALE2 = LOG2E / math.sqrt(DH)
F32 = jnp.float32
BF16 = jnp.bfloat16

NX, NZ, NC = 4, 4, 2
NH, NY = 2, 4


def blk_perm(dx=0, dz=0, dc=0):
    pairs = []
    for x in range(NX):
        for z in range(NZ):
            for c in range(NC):
                there = ((x + dx) % NX * NZ + (z + dz) % NZ) * NC + (c + dc) % NC
                pairs.append(((x * NZ + z) * NC + c, there))
    return pairs


def tensor_perm(dh=0, dy=0):
    return [
        (h * NY + y, (h + dh) % NH * NY + (y + dy) % NY) for h in range(NH) for y in range(NY)
    ]


def params(mib):
    return pltpu.CompilerParams(vmem_limit_bytes=mib << 20)


def cost(micros):
    return pl.CostEstimate(flops=int(micros * 1.1e9), bytes_accessed=1 << 20, transcendentals=0)


def heads_of(q):
    return jnp.concatenate([q[:, h * DH : (h + 1) * DH] for h in range(GROUP)], axis=0)


SUB = 16


def suffix_kernel(len_ref, q_ref, k_ref, v_ref, o_ref, lse_ref):
    rows, slots, _ = k_ref.shape
    row = lax.broadcasted_iota(jnp.int32, (SUB, slots), 0)
    col = lax.broadcasted_iota(jnp.int32, (SUB, slots), 1)
    lane = lax.broadcasted_iota(jnp.int32, (SUB, DH), 1)
    for first in range(0, rows, SUB):
        here = slice(first, first + SUB)
        q = heads_of(q_ref[here, :])
        k = k_ref[here].reshape(SUB * slots, DH)
        v = v_ref[here].reshape(SUB * slots, DH)
        s = lax.dot_general(q, k, (((1,), (1,)), ((), ())), preferred_element_type=F32)
        tiles = [(row == j) & (col < len_ref[first + j]) for j in range(SUB)]
        live = jnp.concatenate(tiles, axis=1)
        live = jnp.concatenate([live] * GROUP, axis=0)
        s = jnp.where(live, s * SCALE2, -jnp.inf)
        peak = jnp.max(s, axis=1, keepdims=True)
        p = jnp.exp2(s - peak)
        total = jnp.sum(p, axis=1, keepdims=True)
        mixed = jnp.dot(p.astype(BF16), v, preferred_element_type=F32) / total
        lse = peak + jnp.log2(total)
        stat = jnp.zeros((SUB, DH), F32)
        for h in range(GROUP):
            o_ref[here, h * DH : (h + 1) * DH] = mixed[h * SUB : (h + 1) * SUB]
            stat = jnp.where(lane == h, lse[h * SUB : (h + 1) * SUB], stat)
        lse_ref[here, :] = stat


def in_vmem(n):
    return [pl.BlockSpec(memory_space=pltpu.VMEM)] * n


def suffix_partial(q, sk, sv, lengths):
    rows = q.shape[0]
    return pl.pallas_call(
        suffix_kernel,
        in_specs=[pl.BlockSpec(memory_space=pltpu.SMEM)] + in_vmem(3),
        out_specs=in_vmem(2),
        out_shape=[
            jax.ShapeDtypeStruct((rows, WIDTH), F32),
            jax.ShapeDtypeStruct((rows, DH), F32),
        ],
        compiler_params=params(12),
        cost_estimate=cost(3.0),
    )(lengths, q, sk, sv)


def stack_kernel(a_ref, b_ref, o_ref, sems):
    rows = a_ref.shape[0]
    copies = [
        pltpu.make_async_copy(ref, o_ref.at[pl.ds(i * rows, rows)], sems.at[i])
        for i, ref in enumerate((a_ref, b_ref))
    ]
    for copy in copies:
        copy.start()
    for copy in copies:
        copy.wait()


def stacked(a, b):
    rows, width = a.shape
    return pl.pallas_call(
        stack_kernel,
        in_specs=[pl.BlockSpec(memory_space=pl.ANY)] * 2,
        out_specs=pl.BlockSpec(memory_space=pltpu.VMEM),
        out_shape=jax.ShapeDtypeStruct((2 * rows, width), a.dtype),
        scratch_shapes=[pltpu.SemaphoreType.DMA((2,))],
        compiler_params=params(4),
        cost_estimate=cost(0.8),
    )(a, b)


def prefix_kernel(groups, half, kinds, old, joined, packed, skip, *refs):
    refs = list(refs)
    qs = [refs.pop(0) for _ in range(groups)]
    kvs = []
    for kind in kinds:
        if kind == "pair":
            kvs.append((refs.pop(0), 0, refs.pop(0), 0))
        else:
            both = refs.pop(0)
            kvs.append((both, 0, both, both.shape[0] // 2))
    if old:
        acc_in, stat_in = refs.pop(0), refs.pop(0)
    if joined:
        part_ref = refs.pop(0)
    rows = qs[0].shape[0] // 2
    total_rows = GROUP * rows
    lane = lax.broadcasted_iota(jnp.int32, (total_rows, DH), 1)
    for g in range(groups):
        q = heads_of(qs[g][half * rows : (half + 1) * rows, :])
        peak = None
        if old:
            span = slice((skip + g) * total_rows, (skip + g + 1) * total_rows)
            acc = acc_in[span, :]
            peak = stat_in[span, 0:1]
            total = stat_in[span, DH // 2 : DH // 2 + 1]
        for k_ref, k_at, v_ref, v_at in kvs:
            size = v_ref.shape[0] - v_at
            k = k_ref[k_at : k_at + size, :]
            v = v_ref[v_at : v_at + size, :]
            s = lax.dot_general(q, k, (((1,), (1,)), ((), ())), preferred_element_type=F32)
            top = jnp.max(s, axis=1, keepdims=True) * SCALE2
            new = top if peak is None else jnp.maximum(peak, top)
            p = jnp.exp2(s * SCALE2 - new).astype(BF16)
            both = jnp.dot(
                p,
                jnp.concatenate([v, jnp.ones_like(v)], axis=1),
                preferred_element_type=F32,
            )
            if peak is None:
                acc, total = both[:, :DH], both[:, DH : DH + 1]
            else:
                fade = jnp.exp2(peak - new)
                acc = acc * fade + both[:, :DH]
                total = total * fade + both[:, DH : DH + 1]
            peak = new
        if joined:
            part = part_ref[(skip + g) * rows : (skip + g + 1) * rows, :]
            logs = jnp.concatenate(logs_of(part), axis=0)
            new = jnp.maximum(peak, logs)
            fade, weight = jnp.exp2(peak - new), jnp.exp2(logs - new)
            acc = acc * fade + heads_of(part).astype(F32) * weight
            total = total * fade + weight
            peak = new
        if packed:
            o_ref, top_row = (refs[0], g * rows) if packed == "one" else (refs[g], 0)
            out = slice(top_row, top_row + rows)
            mixed = (acc / total).astype(BF16)
            lse = peak + jnp.log2(total)
            stat = jnp.zeros((rows, DH), F32)
            for h in range(GROUP):
                part = slice(h * rows, (h + 1) * rows)
                o_ref[out, h * DH : (h + 1) * DH] = mixed[part]
                rest = lse[part]
                for j in range(3):
                    piece = rest.astype(BF16).astype(F32)
                    rest = rest - piece
                    stat = jnp.where(lane[:rows] == 3 * h + j, piece, stat)
            o_ref[out, WIDTH:] = stat.astype(BF16)
        else:
            span = slice(g * total_rows, (g + 1) * total_rows)
            refs[0][span, :] = acc
            refs[1][span, :] = jnp.where(lane < DH // 2, peak, total)


def logs_of(part):
    stat = part[:, WIDTH:].astype(F32)
    logs = []
    for h in range(GROUP):
        at = 3 * h
        logs.append(stat[:, at : at + 1] + stat[:, at + 1 : at + 2] + stat[:, at + 2 : at + 3])
    return logs


def prefix_partial(queries, half, blocks, state=None, part=None, packed=None, skip=0):
    rows = queries[0].shape[0] // 2
    groups = len(queries)
    all_rows = groups * GROUP * rows
    kinds, arrays, keys = [], [], 0
    for block in blocks:
        if isinstance(block, tuple):
            kinds.append("pair")
            arrays += list(block)
            keys += block[0].shape[0]
        else:
            kinds.append("both")
            arrays.append(block)
            keys += block.shape[0] // 2
    arrays = list(queries) + arrays
    if state is not None:
        arrays += list(state)
    if part is not None:
        arrays.append(part)
    if packed == "one":
        outs = [jax.ShapeDtypeStruct((groups * rows, WIDTH + DH), BF16)]
    elif packed:
        outs = [jax.ShapeDtypeStruct((rows, WIDTH + DH), BF16)] * groups
    else:
        outs = [jax.ShapeDtypeStruct((all_rows, DH), F32)] * 2
    kernel = functools.partial(
        prefix_kernel,
        groups,
        half,
        tuple(kinds),
        state is not None,
        part is not None,
        packed,
        skip,
    )
    return pl.pallas_call(
        kernel,
        in_specs=in_vmem(len(arrays)),
        out_specs=in_vmem(len(outs)),
        out_shape=outs,
        compiler_params=params(16),
        cost_estimate=cost(0.5 + 1.4e-6 * all_rows * keys),
    )(*arrays)


def merged(parts, mixed, lse):
    columns = []
    for h in range(GROUP):
        span = slice(h * DH, (h + 1) * DH)
        logs, values = [lse[:, h : h + 1]], [mixed[:, span]]
        for part in parts:
            logs.append(logs_of(part)[h])
            values.append(part[:, span].astype(F32))
        peak = functools.reduce(jnp.maximum, logs)
        weights = [jnp.exp2(log - peak) for log in logs]
        total = functools.reduce(jnp.add, weights)
        value = functools.reduce(jnp.add, [w * o for w, o in zip(weights, values)])
        columns.append((value / total).astype(BF16))
    return jnp.concatenate(columns, axis=1)


def project_kernel(first, merge, index_ref, weight_ref, *refs):
    refs = list(refs)
    piece = weight_ref.shape[1] // (NH * NY)
    if merge:
        *parts, mixed, lse = refs[: NZ + 2]
        *outs, att_ref = refs[NZ + 2 :]
        att = merged([p[...] for p in parts], mixed[...], lse[...])
        att_ref[...] = att
    else:
        att = refs[0][...]
        outs = refs[1:]
    for k, o in enumerate(outs):
        at = pl.multiple_of(index_ref[first + k] * piece, piece)
        w = weight_ref[:, pl.ds(at, piece)]
        o[...] = jnp.dot(att, w, preferred_element_type=F32).astype(o.dtype)


def project(index, first, inputs, weight, merge):
    rows = inputs[0].shape[0]
    depth, columns = weight.shape
    piece = columns // (NH * NY)
    outs = [jax.ShapeDtypeStruct((rows, piece), F32 if k == 0 else BF16) for k in range(NY)]
    if merge:
        outs.append(jax.ShapeDtypeStruct((rows, depth), BF16))
    return pl.pallas_call(
        functools.partial(project_kernel, first, merge),
        in_specs=[pl.BlockSpec(memory_space=pltpu.SMEM)] + in_vmem(1 + len(inputs)),
        out_specs=in_vmem(len(outs)),
        out_shape=outs,
        compiler_params=params(16),
        cost_estimate=cost(3.0),
    )(index, weight, *inputs)


def on_device(
    queries, prefix_keys, prefix_values, suffix_keys, suffix_values, suffix_lengths, out_weight
):
    here = lax.axis_index("tensor").astype(jnp.int32)
    step = jnp.arange(NH * NY, dtype=jnp.int32)
    index = (here + NY * (1 - step // NY)) // NY % NH * NY + (here + step) % NY

    send = functools.partial(lax.ppermute, axis_name="blk")
    far_queries = send(queries, perm=blk_perm(dx=2))
    both = stacked(prefix_keys, prefix_values)
    peer = send(both, perm=blk_perm(dc=1))
    near = [send(both, perm=blk_perm(dx=d)) for d in (1, 3)]
    pair = stacked(queries, far_queries)
    group = [pair] + [send(pair, perm=blk_perm(dz=d)) for d in (1, 2, 3)]

    together = lax.optimization_barrier
    peer, index = together((peer, index))
    mine = [(prefix_keys, prefix_values), peer]
    (far_part,) = prefix_partial(group, 1, mine, packed="one")
    near, far_part = together((near, far_part))
    far_part = send(far_part, perm=blk_perm(dx=2))
    near_peer = [send(b, perm=blk_perm(dc=1)) for b in near]
    state = prefix_partial(group, 0, mine)
    state = prefix_partial(group, 0, near, state)
    near_peer, state = together((near_peer, state))
    away = prefix_partial(group[1:], 0, near_peer, state, far_part, "each", 1)

    suffix_lengths, state, away = together((suffix_lengths, state, away))
    away = [send(part, perm=blk_perm(dz=-d)) for d, part in enumerate(away, 1)]
    home = prefix_partial(group[:1], 0, near_peer, state, far_part, "each")
    mixed, lse = suffix_partial(queries, suffix_keys, suffix_values, suffix_lengths)
    parts = list(home) + away

    send = functools.partial(lax.ppermute, axis_name="tensor")
    *away, attention = project(index, 0, parts + [mixed, lse], out_weight, True)
    away = [away[0]] + [send(away[d], perm=tensor_perm(dy=d)) for d in (1, 2, 3)]
    home = project(index, NY, [attention], out_weight, False)
    home = [home[0]] + [send(home[d], perm=tensor_perm(dy=d)) for d in (1, 2, 3)]

    def summed(pieces):
        return functools.reduce(jnp.add, [p.astype(F32) for p in pieces])

    other = send(summed(away).astype(BF16), perm=tensor_perm(dh=1))
    return summed(home + [other]).astype(BF16)


def solution(mesh):
    in_specs = (
        P("blk", "tensor"),
        P("blk", "tensor"),
        P("blk", "tensor"),
        P("blk", None, "tensor"),
        P("blk", None, "tensor"),
        P("blk"),
        P("tensor", None),
    )
    out_specs = P("blk", "tensor")
    return jax.shard_map(
        on_device, mesh=mesh, in_specs=in_specs, out_specs=out_specs, check_vma=False
    )
```

```python
import functools
import math

import jax
import jax.numpy as jnp
from jax import lax
from jax.experimental import pallas as pl
from jax.experimental.pallas import tpu as pltpu
from jax.sharding import PartitionSpec as P

DH = 128
GROUP = 4
WIDTH = GROUP * DH
LOG2E = math.log2(math.e)
SCALE2 = LOG2E / math.sqrt(DH)
F32 = jnp.float32
BF16 = jnp.bfloat16

NX, NZ, NC = 4, 4, 2
NH, NY = 2, 4


def blk_perm(dx=0, dz=0, dc=0):
    pairs = []
    for x in range(NX):
        for z in range(NZ):
            for c in range(NC):
                there = ((x + dx) % NX * NZ + (z + dz) % NZ) * NC + (c + dc) % NC
                pairs.append(((x * NZ + z) * NC + c, there))
    return pairs


def tensor_perm(dh=0, dy=0):
    return [
        (h * NY + y, (h + dh) % NH * NY + (y + dy) % NY) for h in range(NH) for y in range(NY)
    ]


def params(mib):
    return pltpu.CompilerParams(vmem_limit_bytes=mib << 20)


def cost(micros):
    return pl.CostEstimate(flops=int(micros * 1.1e9), bytes_accessed=1 << 20, transcendentals=0)


def heads_of(q):
    return jnp.concatenate([q[:, h * DH : (h + 1) * DH] for h in range(GROUP)], axis=0)


SUB = 16


def suffix_kernel(len_ref, q_ref, k_ref, v_ref, o_ref, lse_ref):
    rows, slots, _ = k_ref.shape
    row = lax.broadcasted_iota(jnp.int32, (SUB, slots), 0)
    col = lax.broadcasted_iota(jnp.int32, (SUB, slots), 1)
    for first in range(0, rows, SUB):
        here = slice(first, first + SUB)
        q = heads_of(q_ref[here, :])
        k = k_ref[here].reshape(SUB * slots, DH)
        v = v_ref[here].reshape(SUB * slots, DH)
        s = lax.dot_general(q, k, (((1,), (1,)), ((), ())), preferred_element_type=F32)
        tiles = [(row == j) & (col < len_ref[first + j]) for j in range(SUB)]
        live = jnp.concatenate(tiles, axis=1)
        live = jnp.concatenate([live] * GROUP, axis=0)
        s = jnp.where(live, s * SCALE2, -jnp.inf)
        peak = jnp.max(s, axis=1, keepdims=True)
        p = jnp.exp2(s - peak)
        total = jnp.sum(p, axis=1, keepdims=True)
        mixed = jnp.dot(p.astype(BF16), v, preferred_element_type=F32) / total
        lse = peak + jnp.log2(total)
        for h in range(GROUP):
            part = slice(h * SUB, (h + 1) * SUB)
            o_ref[here, h * DH : (h + 1) * DH] = mixed[part]
            lse_ref[here, h * DH : (h + 1) * DH] = jnp.broadcast_to(lse[part], (SUB, DH))


def in_vmem(n):
    return [pl.BlockSpec(memory_space=pltpu.VMEM)] * n


def suffix_partial(q, sk, sv, lengths):
    rows = q.shape[0]
    return pl.pallas_call(
        suffix_kernel,
        in_specs=[pl.BlockSpec(memory_space=pltpu.SMEM)] + in_vmem(3),
        out_specs=in_vmem(2),
        out_shape=[jax.ShapeDtypeStruct((rows, WIDTH), F32)] * 2,
        compiler_params=params(12),
        cost_estimate=cost(3.0),
    )(lengths, q, sk, sv)


def stack_kernel(pieces, a_ref, b_ref, o_ref, sems):
    rows = a_ref.shape[0]
    step = rows // pieces
    copies = []
    for i, ref in enumerate((a_ref, b_ref)):
        for j in range(pieces):
            n = i * pieces + j
            copies.append(
                pltpu.make_async_copy(
                    ref.at[pl.ds(j * step, step)], o_ref.at[pl.ds(n * step, step)], sems.at[n]
                )
            )
    for copy in copies:
        copy.start()
    for copy in copies:
        copy.wait()


def stacked(a, b, pieces, mib):
    rows, width = a.shape
    return pl.pallas_call(
        functools.partial(stack_kernel, pieces),
        in_specs=[pl.BlockSpec(memory_space=pl.ANY)] * 2,
        out_specs=pl.BlockSpec(memory_space=pltpu.VMEM),
        out_shape=jax.ShapeDtypeStruct((2 * rows, width), a.dtype),
        scratch_shapes=[pltpu.SemaphoreType.DMA((2 * pieces,))],
        compiler_params=params(mib),
        cost_estimate=cost(0.8),
    )(a, b)


def spread(part):
    row = lax.broadcasted_iota(jnp.int32, (DH, WIDTH), 0)
    col = lax.broadcasted_iota(jnp.int32, (DH, WIDTH), 1)
    chosen = jnp.zeros((DH, WIDTH), F32)
    for h in range(GROUP):
        mine = (row >= 3 * h) & (row < 3 * h + 3) & (col >= h * DH) & (col < (h + 1) * DH)
        chosen = jnp.where(mine, 1.0, chosen)
    return jnp.dot(part[:, WIDTH:], chosen.astype(BF16), preferred_element_type=F32)


def pack(o_ref, out, values, logs):
    rows = values.shape[0] // GROUP
    lane = lax.broadcasted_iota(jnp.int32, (rows, DH), 1)
    stat = jnp.zeros((rows, DH), F32)
    for h in range(GROUP):
        span = slice(h * rows, (h + 1) * rows)
        o_ref[out, h * DH : (h + 1) * DH] = values[span].astype(BF16)
        rest = logs[span]
        for j in range(3):
            piece = rest.astype(BF16).astype(F32)
            rest = rest - piece
            stat = jnp.where(lane == 3 * h + j, piece, stat)
    o_ref[out, WIDTH:] = stat.astype(BF16)


def locate(counts, at):
    for i, count in enumerate(counts):
        if at < count:
            return i, at
        at -= count


def prefix_kernel(groups, half, blocks, olds, joins, packed, skip, *refs):
    refs = list(refs)

    def take(n):
        return [refs.pop(0) for _ in range(n)]

    qs, kvs = take(groups), take(blocks)
    old_refs, part_refs = take(2 * len(olds)), take(len(joins))
    rows = qs[0].shape[0] // 2
    size = kvs[0].shape[0] // 2
    many = GROUP * rows

    def scores(g, b):
        q = heads_of(qs[g][half * rows : (half + 1) * rows, :])
        return lax.dot_general(
            q, kvs[b][:size, :], (((1,), (1,)), ((), ())), preferred_element_type=F32
        )

    units = [(g, b) for g in range(groups) for b in range(blocks)]
    ahead = scores(*units[0])
    for at, (g, b) in enumerate(units):
        s = ahead
        if at + 1 < len(units):
            ahead = scores(*units[at + 1])
        if b == 0:
            peak = None
            if olds:
                i, n = locate(olds, skip + g)
                span = slice(n * many, (n + 1) * many)
                both = old_refs[2 * i][span, :]
                peak = old_refs[2 * i + 1][span, 0:1]
        top = jnp.max(s, axis=1, keepdims=True) * SCALE2
        new = top if peak is None else jnp.maximum(peak, top)
        p = jnp.exp2(s * SCALE2 - new).astype(BF16)
        v = kvs[b][size:, :]
        added = jnp.dot(
            p, jnp.concatenate([v, jnp.ones_like(v)], axis=1), preferred_element_type=F32
        )
        both = added if peak is None else both * jnp.exp2(peak - new) + added
        peak = new
        if b < blocks - 1:
            continue
        level = jnp.broadcast_to(peak, (many, DH))
        if not packed:
            span = slice(g * many, (g + 1) * many)
            refs[0][span, :] = both
            refs[1][span, :] = level
            continue
        acc, total = both[:, :DH], both[:, DH:]
        if joins:
            i, n = locate(joins, skip + g)
            part = part_refs[i][n * rows : (n + 1) * rows, :]
            logs = heads_of(spread(part))
            new = jnp.maximum(level, logs)
            fade, weight = jnp.exp2(level - new), jnp.exp2(logs - new)
            acc = acc * fade + heads_of(part).astype(F32) * weight
            total = total * fade + weight
            level = new
        o_ref, first = (refs[0], g * rows) if packed == "one" else (refs[g], 0)
        pack(o_ref, slice(first, first + rows), acc / total, level + jnp.log2(total))


def prefix_partial(queries, half, blocks, olds=(), joins=(), packed=None, skip=0):
    rows = queries[0].shape[0] // 2
    groups = len(queries)
    many = GROUP * rows
    keys = sum(b.shape[0] // 2 for b in blocks)
    arrays = [*queries, *blocks, *(a for old in olds for a in old), *joins]
    if packed == "one":
        outs = [jax.ShapeDtypeStruct((groups * rows, WIDTH + DH), BF16)]
    elif packed:
        outs = [jax.ShapeDtypeStruct((rows, WIDTH + DH), BF16)] * groups
    else:
        outs = [jax.ShapeDtypeStruct((groups * many, n * DH), F32) for n in (2, 1)]
    kernel = functools.partial(
        prefix_kernel,
        groups,
        half,
        len(blocks),
        [old[0].shape[0] // many for old in olds],
        [part.shape[0] // rows for part in joins],
        packed,
        skip,
    )
    return pl.pallas_call(
        kernel,
        in_specs=in_vmem(len(arrays)),
        out_specs=in_vmem(len(outs)),
        out_shape=outs,
        compiler_params=params(16),
        cost_estimate=cost(0.5 + 1.4e-6 * groups * many * keys),
    )(*arrays)


def merged(parts, mixed, lse):
    logs = [lse] + [spread(part) for part in parts]
    values = [mixed] + [part[:, :WIDTH].astype(F32) for part in parts]
    peak = functools.reduce(jnp.maximum, logs)
    weights = [jnp.exp2(log - peak) for log in logs]
    total = functools.reduce(jnp.add, weights)
    value = functools.reduce(jnp.add, [w * o for w, o in zip(weights, values)])
    return (value / total).astype(BF16)


def project_kernel(first, merge, index_ref, weight_ref, *refs):
    refs = list(refs)
    piece = weight_ref.shape[1] // (NH * NY)
    if merge:
        *parts, mixed, lse = refs[: NZ + 2]
        *outs, att_ref = refs[NZ + 2 :]
        att = merged([p[...] for p in parts], mixed[...], lse[...])
        att_ref[...] = att
    else:
        att = refs[0][...]
        outs = refs[1:]
    for k, o in enumerate(outs):
        at = pl.multiple_of(index_ref[first + k] * piece, piece)
        w = weight_ref[:, pl.ds(at, piece)]
        o[...] = jnp.dot(att, w, preferred_element_type=F32).astype(o.dtype)


def project(index, first, inputs, weight, merge):
    rows = inputs[0].shape[0]
    depth, columns = weight.shape
    piece = columns // (NH * NY)
    outs = [jax.ShapeDtypeStruct((rows, piece), F32 if k == 0 else BF16) for k in range(NY)]
    if merge:
        outs.append(jax.ShapeDtypeStruct((rows, depth), BF16))
    return pl.pallas_call(
        functools.partial(project_kernel, first, merge),
        in_specs=[pl.BlockSpec(memory_space=pltpu.SMEM)] + in_vmem(1 + len(inputs)),
        out_specs=in_vmem(len(outs)),
        out_shape=outs,
        compiler_params=params(16),
        cost_estimate=cost(3.0),
    )(index, weight, *inputs)


def on_device(
    queries, prefix_keys, prefix_values, suffix_keys, suffix_values, suffix_lengths, out_weight
):
    here = lax.axis_index("tensor").astype(jnp.int32)
    step = jnp.arange(NH * NY, dtype=jnp.int32)
    index = (here + NY * (1 - step // NY)) // NY % NH * NY + (here + step) % NY

    send = functools.partial(lax.ppermute, axis_name="blk")
    far_queries = send(queries, perm=blk_perm(dx=2))
    own = stacked(prefix_keys, prefix_values, 4, 56)
    peer = send(own, perm=blk_perm(dc=1))
    near = [send(own, perm=blk_perm(dx=d)) for d in (1, 3)]
    pair = stacked(queries, far_queries, 1, 4)
    shifts = (0, 3, 1, 2)
    group = [pair] + [send(pair, perm=blk_perm(dz=d)) for d in shifts[1:]]

    together = lax.optimization_barrier
    mixed, lse = suffix_partial(queries, suffix_keys, suffix_values, suffix_lengths)
    peer, index, lse = together((peer, index, lse))
    chip = [own, peer]
    (part_a,) = prefix_partial(group[:2], 1, chip, packed="one")
    part_a = send(part_a, perm=blk_perm(dx=2))
    state_a = prefix_partial(group[:2], 0, chip)
    rest, state_a = together((group[2:], state_a))
    group = group[:2] + rest
    (part_b,) = prefix_partial(rest, 1, chip, packed="one")
    near, part_b = together((near, part_b))
    part_b = send(part_b, perm=blk_perm(dx=2))
    near_peer = [send(b, perm=blk_perm(dc=1)) for b in near]
    state_b = prefix_partial(rest, 0, chip)
    state = prefix_partial(group, 0, near, [state_a, state_b])
    near_peer, state = together((near_peer, state))
    joins = [part_a, part_b]
    (third,) = prefix_partial(group[3:], 0, near_peer, [state], joins, "each", 3)
    state, third = together((state, third))
    away = prefix_partial(group[1:3], 0, near_peer, [state], joins, "each", 1)
    state, away = together((state, away))
    away = [send(part, perm=blk_perm(dz=-d)) for d, part in zip(shifts[1:], [*away, third])]
    home = prefix_partial(group[:1], 0, near_peer, [state], joins, "each")
    parts = [*home, *away]

    send = functools.partial(lax.ppermute, axis_name="tensor")
    *away, attention = project(index, 0, parts + [mixed, lse], out_weight, True)
    away = [away[0]] + [send(away[d], perm=tensor_perm(dy=d)) for d in (1, 2, 3)]
    home = project(index, NY, [attention], out_weight, False)
    home = [home[0]] + [send(home[d], perm=tensor_perm(dy=d)) for d in (1, 2, 3)]

    def summed(pieces):
        return functools.reduce(jnp.add, [p.astype(F32) for p in pieces])

    other = send(summed(away).astype(BF16), perm=tensor_perm(dh=1))
    return summed(home + [other]).astype(BF16)


def solution(mesh):
    in_specs = (
        P("blk", "tensor"),
        P("blk", "tensor"),
        P("blk", "tensor"),
        P("blk", None, "tensor"),
        P("blk", None, "tensor"),
        P("blk"),
        P("tensor", None),
    )
    out_specs = P("blk", "tensor")
    return jax.shard_map(
        on_device, mesh=mesh, in_specs=in_specs, out_specs=out_specs, check_vma=False
    )
```

```python
import functools
import math

import jax
import jax.numpy as jnp
from jax import lax
from jax.experimental import pallas as pl
from jax.experimental.pallas import tpu as pltpu
from jax.sharding import PartitionSpec as P

DH = 128
GROUP = 4
WIDTH = GROUP * DH
LOG2E = math.log2(math.e)
SCALE2 = LOG2E / math.sqrt(DH)
F32 = jnp.float32
BF16 = jnp.bfloat16

NX, NZ, NC = 4, 4, 2
NH, NY = 2, 4


def blk_perm(dx=0, dz=0, dc=0):
    pairs = []
    for x in range(NX):
        for z in range(NZ):
            for c in range(NC):
                there = ((x + dx) % NX * NZ + (z + dz) % NZ) * NC + (c + dc) % NC
                pairs.append(((x * NZ + z) * NC + c, there))
    return pairs


def tensor_perm(dh=0, dy=0):
    return [
        (h * NY + y, (h + dh) % NH * NY + (y + dy) % NY) for h in range(NH) for y in range(NY)
    ]


def params(mib):
    return pltpu.CompilerParams(vmem_limit_bytes=mib << 20)


def cost(micros):
    return pl.CostEstimate(flops=int(micros * 1.1e9), bytes_accessed=1 << 20, transcendentals=0)


def heads_of(q):
    return jnp.concatenate([q[:, h * DH : (h + 1) * DH] for h in range(GROUP)], axis=0)


SUB = 16


def suffix_kernel(len_ref, q_ref, k_ref, v_ref, o_ref, lse_ref):
    rows, slots, _ = k_ref.shape
    row = lax.broadcasted_iota(jnp.int32, (SUB, slots), 0)
    col = lax.broadcasted_iota(jnp.int32, (SUB, slots), 1)
    for first in range(0, rows, SUB):
        here = slice(first, first + SUB)
        q = heads_of(q_ref[here, :])
        k = k_ref[here].reshape(SUB * slots, DH)
        v = v_ref[here].reshape(SUB * slots, DH)
        s = lax.dot_general(q, k, (((1,), (1,)), ((), ())), preferred_element_type=F32)
        tiles = [(row == j) & (col < len_ref[first + j]) for j in range(SUB)]
        live = jnp.concatenate(tiles, axis=1)
        live = jnp.concatenate([live] * GROUP, axis=0)
        s = jnp.where(live, s * SCALE2, -jnp.inf)
        peak = jnp.max(s, axis=1, keepdims=True)
        p = jnp.exp2(s - peak)
        total = jnp.sum(p, axis=1, keepdims=True)
        mixed = jnp.dot(p.astype(BF16), v, preferred_element_type=F32) / total
        lse = peak + jnp.log2(total)
        for h in range(GROUP):
            part = slice(h * SUB, (h + 1) * SUB)
            there = slice(h * rows + first, h * rows + first + SUB)
            o_ref[there, :] = mixed[part]
            lse_ref[there, :] = jnp.broadcast_to(lse[part], (SUB, DH))


def in_vmem(n):
    return [pl.BlockSpec(memory_space=pltpu.VMEM)] * n


def suffix_partial(q, sk, sv, lengths):
    rows = q.shape[0]
    return pl.pallas_call(
        suffix_kernel,
        in_specs=[pl.BlockSpec(memory_space=pltpu.SMEM)] + in_vmem(3),
        out_specs=in_vmem(2),
        out_shape=[jax.ShapeDtypeStruct((GROUP * rows, DH), F32)] * 2,
        compiler_params=params(12),
        cost_estimate=cost(3.0),
    )(lengths, q, sk, sv)


def stack_kernel(pieces, a_ref, b_ref, o_ref, sems):
    rows = a_ref.shape[0]
    step = rows // pieces
    copies = []
    for i, ref in enumerate((a_ref, b_ref)):
        for j in range(pieces):
            n = i * pieces + j
            copies.append(
                pltpu.make_async_copy(
                    ref.at[pl.ds(j * step, step)], o_ref.at[pl.ds(n * step, step)], sems.at[n]
                )
            )
    for copy in copies:
        copy.start()
    for copy in copies:
        copy.wait()


def stacked(a, b, pieces, mib):
    rows, width = a.shape
    return pl.pallas_call(
        functools.partial(stack_kernel, pieces),
        in_specs=[pl.BlockSpec(memory_space=pl.ANY)] * 2,
        out_specs=pl.BlockSpec(memory_space=pltpu.VMEM),
        out_shape=jax.ShapeDtypeStruct((2 * rows, width), a.dtype),
        scratch_shapes=[pltpu.SemaphoreType.DMA((2 * pieces,))],
        compiler_params=params(mib),
        cost_estimate=cost(0.8),
    )(a, b)


TILE = 16


def spread(part):
    rows = (part.shape[0] - TILE) // GROUP
    count = GROUP * rows // TILE
    row = lax.broadcasted_iota(jnp.int32, (DH, count * DH), 0)
    first = 3 * lax.shift_right_logical(
        lax.broadcasted_iota(jnp.int32, (DH, count * DH), 1), DH.bit_length() - 1
    )
    chosen = jnp.where((row >= first) & (row < first + 3), 1.0, 0.0).astype(BF16)
    logs = jnp.dot(part[GROUP * rows :, :], chosen, preferred_element_type=F32)
    order = [n * GROUP + h for h in range(GROUP) for n in range(rows // TILE)]
    return jnp.concatenate([logs[:, n * DH : (n + 1) * DH] for n in order], axis=0)


def pack(o_ref, first, values, logs):
    many = values.shape[0]
    rows = many // GROUP
    o_ref[first : first + many, :] = values.astype(BF16)
    lane = lax.broadcasted_iota(jnp.int32, (TILE, DH), 1)
    strip = jnp.zeros((TILE, DH), F32)
    for n in range(rows // TILE):
        for h in range(GROUP):
            rest = logs[h * rows + n * TILE : h * rows + (n + 1) * TILE]
            for j in range(3):
                piece = rest.astype(BF16).astype(F32)
                rest = rest - piece
                strip = jnp.where(lane == 3 * (n * GROUP + h) + j, piece, strip)
    o_ref[first + many : first + many + TILE, :] = strip.astype(BF16)


def locate(counts, at):
    for i, count in enumerate(counts):
        if at < count:
            return i, at
        at -= count


def prefix_kernel(groups, half, blocks, olds, joins, packed, skip, *refs):
    refs = list(refs)

    def take(n):
        return [refs.pop(0) for _ in range(n)]

    qs, kvs = take(groups), take(blocks)
    old_refs, part_refs = take(2 * len(olds)), take(len(joins))
    rows = qs[0].shape[0] // 2
    size = kvs[0].shape[0] // 2
    many = GROUP * rows

    def scores(g, b):
        q = heads_of(qs[g][half * rows : (half + 1) * rows, :])
        return lax.dot_general(
            q, kvs[b][:size, :], (((1,), (1,)), ((), ())), preferred_element_type=F32
        )

    units = [(g, b) for g in range(groups) for b in range(blocks)]
    ahead = scores(*units[0])
    for at, (g, b) in enumerate(units):
        s = ahead
        if at + 1 < len(units):
            ahead = scores(*units[at + 1])
        if b == 0:
            peak = None
            if olds:
                i, n = locate(olds, skip + g)
                span = slice(n * many, (n + 1) * many)
                both = old_refs[2 * i][span, :]
                peak = old_refs[2 * i + 1][span, 0:1]
        top = jnp.max(s, axis=1, keepdims=True) * SCALE2
        new = top if peak is None else jnp.maximum(peak, top)
        p = jnp.exp2(s * SCALE2 - new).astype(BF16)
        v = kvs[b][size:, :]
        added = jnp.dot(
            p, jnp.concatenate([v, jnp.ones_like(v)], axis=1), preferred_element_type=F32
        )
        both = added if peak is None else both * jnp.exp2(peak - new) + added
        peak = new
        if b < blocks - 1:
            continue
        level = jnp.broadcast_to(peak, (many, DH))
        if not packed:
            span = slice(g * many, (g + 1) * many)
            refs[0][span, :] = both
            refs[1][span, :] = level
            continue
        acc, total = both[:, :DH], both[:, DH:]
        if joins:
            i, n = locate(joins, skip + g)
            part = part_refs[i][n * (many + TILE) : (n + 1) * (many + TILE), :]
            logs = spread(part)
            new = jnp.maximum(level, logs)
            fade, weight = jnp.exp2(level - new), jnp.exp2(logs - new)
            acc = acc * fade + part[:many, :].astype(F32) * weight
            total = total * fade + weight
            level = new
        o_ref, first = (refs[0], g * (many + TILE)) if packed == "one" else (refs[g], 0)
        pack(o_ref, first, acc / total, level + jnp.log2(total))


def prefix_partial(queries, half, blocks, olds=(), joins=(), packed=None, skip=0):
    rows = queries[0].shape[0] // 2
    groups = len(queries)
    many = GROUP * rows
    keys = sum(b.shape[0] // 2 for b in blocks)
    arrays = [*queries, *blocks, *(a for old in olds for a in old), *joins]
    if packed == "one":
        outs = [jax.ShapeDtypeStruct((groups * (many + TILE), DH), BF16)]
    elif packed:
        outs = [jax.ShapeDtypeStruct((many + TILE, DH), BF16)] * groups
    else:
        outs = [jax.ShapeDtypeStruct((groups * many, n * DH), F32) for n in (2, 1)]
    kernel = functools.partial(
        prefix_kernel,
        groups,
        half,
        len(blocks),
        [old[0].shape[0] // many for old in olds],
        [part.shape[0] // (many + TILE) for part in joins],
        packed,
        skip,
    )
    return pl.pallas_call(
        kernel,
        in_specs=in_vmem(len(arrays)),
        out_specs=in_vmem(len(outs)),
        out_shape=outs,
        compiler_params=params(16),
        cost_estimate=cost(0.5 + 1.4e-6 * groups * many * keys),
    )(*arrays)


def merged(parts, mixed, lse):
    logs = [lse] + [spread(part) for part in parts]
    many = mixed.shape[0]
    rows = many // GROUP
    values = [mixed] + [part[:many, :].astype(F32) for part in parts]
    peak = functools.reduce(jnp.maximum, logs)
    weights = [jnp.exp2(log - peak) for log in logs]
    total = functools.reduce(jnp.add, weights)
    value = functools.reduce(jnp.add, [w * o for w, o in zip(weights, values)])
    value = (value / total).astype(BF16)
    return jnp.concatenate([value[h * rows : (h + 1) * rows] for h in range(GROUP)], axis=1)


def project_kernel(first, merge, index_ref, weight_ref, *refs):
    refs = list(refs)
    piece = weight_ref.shape[1] // (NH * NY)
    if merge:
        *parts, mixed, lse = refs[: NZ + 2]
        *outs, att_ref = refs[NZ + 2 :]
        att = merged([p[...] for p in parts], mixed[...], lse[...])
        att_ref[...] = att
    else:
        att = refs[0][...]
        outs = refs[1:]
    for k, o in enumerate(outs):
        at = pl.multiple_of(index_ref[first + k] * piece, piece)
        w = weight_ref[:, pl.ds(at, piece)]
        o[...] = jnp.dot(att, w, preferred_element_type=F32).astype(o.dtype)


def project(rows, index, first, inputs, weight, merge):
    depth, columns = weight.shape
    piece = columns // (NH * NY)
    outs = [jax.ShapeDtypeStruct((rows, piece), F32 if k == 0 else BF16) for k in range(NY)]
    if merge:
        outs.append(jax.ShapeDtypeStruct((rows, depth), BF16))
    return pl.pallas_call(
        functools.partial(project_kernel, first, merge),
        in_specs=[pl.BlockSpec(memory_space=pltpu.SMEM)] + in_vmem(1 + len(inputs)),
        out_specs=in_vmem(len(outs)),
        out_shape=outs,
        compiler_params=params(16),
        cost_estimate=cost(3.0),
    )(index, weight, *inputs)


def on_device(
    queries, prefix_keys, prefix_values, suffix_keys, suffix_values, suffix_lengths, out_weight
):
    here = lax.axis_index("tensor").astype(jnp.int32)
    step = jnp.arange(NH * NY, dtype=jnp.int32)
    index = (here + NY * (1 - step // NY)) // NY % NH * NY + (here + step) % NY

    send = functools.partial(lax.ppermute, axis_name="blk")
    far_queries = send(queries, perm=blk_perm(dx=2))
    own = stacked(prefix_keys, prefix_values, 4, 56)
    peer = send(own, perm=blk_perm(dc=1))
    near = [send(own, perm=blk_perm(dx=d)) for d in (1, 3)]
    pair = stacked(queries, far_queries, 1, 4)
    shifts = (0, 3, 1, 2)
    group = [pair] + [send(pair, perm=blk_perm(dz=d)) for d in shifts[1:]]

    together = lax.optimization_barrier
    mixed, lse = suffix_partial(queries, suffix_keys, suffix_values, suffix_lengths)
    peer, index, lse = together((peer, index, lse))
    chip = [own, peer]
    (part_a,) = prefix_partial(group[:2], 1, chip, packed="one")
    part_a = send(part_a, perm=blk_perm(dx=2))
    state_a = prefix_partial(group[:2], 0, chip)
    rest, state_a = together((group[2:], state_a))
    group = group[:2] + rest
    (part_b,) = prefix_partial(rest, 1, chip, packed="one")
    near, part_b = together((near, part_b))
    part_b = send(part_b, perm=blk_perm(dx=2))
    near_peer = [send(b, perm=blk_perm(dc=1)) for b in near]
    state_b = prefix_partial(rest, 0, chip)
    state = prefix_partial(group, 0, near, [state_a, state_b])
    near_peer, state = together((near_peer, state))
    joins = [part_a, part_b]
    (third,) = prefix_partial(group[3:], 0, near_peer, [state], joins, "each", 3)
    state, third = together((state, third))
    away = prefix_partial(group[1:3], 0, near_peer, [state], joins, "each", 1)
    state, away = together((state, away))
    away = [send(part, perm=blk_perm(dz=-d)) for d, part in zip(shifts[1:], [*away, third])]
    home = prefix_partial(group[:1], 0, near_peer, [state], joins, "each")
    parts = [*home, *away]

    send = functools.partial(lax.ppermute, axis_name="tensor")
    *away, attention = project(queries.shape[0], index, 0, parts + [mixed, lse], out_weight, True)
    away = [away[0]] + [send(away[d], perm=tensor_perm(dy=d)) for d in (1, 2, 3)]
    home = project(queries.shape[0], index, NY, [attention], out_weight, False)
    home = [home[0]] + [send(home[d], perm=tensor_perm(dy=d)) for d in (1, 2, 3)]

    def summed(pieces):
        return functools.reduce(jnp.add, [p.astype(F32) for p in pieces])

    other = send(summed(away).astype(BF16), perm=tensor_perm(dh=1))
    return summed(home + [other]).astype(BF16)


def solution(mesh):
    in_specs = (
        P("blk", "tensor"),
        P("blk", "tensor"),
        P("blk", "tensor"),
        P("blk", None, "tensor"),
        P("blk", None, "tensor"),
        P("blk"),
        P("tensor", None),
    )
    out_specs = P("blk", "tensor")
    return jax.shard_map(
        on_device, mesh=mesh, in_specs=in_specs, out_specs=out_specs, check_vma=False
    )
```

```python
import functools
import math

import jax
import jax.numpy as jnp
from jax import lax
from jax.experimental import pallas as pl
from jax.experimental.pallas import tpu as pltpu
from jax.sharding import PartitionSpec as P

DH = 128
GROUP = 4
WIDTH = GROUP * DH
LOG2E = math.log2(math.e)
SCALE2 = LOG2E / math.sqrt(DH)
F32 = jnp.float32
BF16 = jnp.bfloat16

NX, NZ, NC = 4, 4, 2
NH, NY = 2, 4


def blk_perm(dx=0, dz=0, dc=0):
    pairs = []
    for x in range(NX):
        for z in range(NZ):
            for c in range(NC):
                there = ((x + dx) % NX * NZ + (z + dz) % NZ) * NC + (c + dc) % NC
                pairs.append(((x * NZ + z) * NC + c, there))
    return pairs


def tensor_perm(dh=0, dy=0):
    return [
        (h * NY + y, (h + dh) % NH * NY + (y + dy) % NY) for h in range(NH) for y in range(NY)
    ]


def params(mib):
    return pltpu.CompilerParams(vmem_limit_bytes=mib << 20)


def cost(micros):
    return pl.CostEstimate(flops=int(micros * 1.1e9), bytes_accessed=1 << 20, transcendentals=0)


def heads_of(q):
    return jnp.concatenate([q[:, h * DH : (h + 1) * DH] for h in range(GROUP)], axis=0)


SUB = 16


def suffix_kernel(len_ref, q_ref, k_ref, v_ref, o_ref, lse_ref):
    rows, slots, _ = k_ref.shape
    row = lax.broadcasted_iota(jnp.int32, (SUB, slots), 0)
    col = lax.broadcasted_iota(jnp.int32, (SUB, slots), 1)
    for first in range(0, rows, SUB):
        here = slice(first, first + SUB)
        q = heads_of(q_ref[here, :])
        k = k_ref[here].reshape(SUB * slots, DH)
        v = v_ref[here].reshape(SUB * slots, DH)
        s = lax.dot_general(q, k, (((1,), (1,)), ((), ())), preferred_element_type=F32)
        tiles = [(row == j) & (col < len_ref[first + j]) for j in range(SUB)]
        live = jnp.concatenate(tiles, axis=1)
        live = jnp.concatenate([live] * GROUP, axis=0)
        s = jnp.where(live, s * SCALE2, -jnp.inf)
        peak = jnp.max(s, axis=1, keepdims=True)
        p = jnp.exp2(s - peak)
        total = jnp.sum(p, axis=1, keepdims=True)
        mixed = jnp.dot(p.astype(BF16), v, preferred_element_type=F32) / total
        lse = peak + jnp.log2(total)
        for h in range(GROUP):
            part = slice(h * SUB, (h + 1) * SUB)
            there = slice(h * rows + first, h * rows + first + SUB)
            o_ref[there, :] = mixed[part]
            lse_ref[there, :] = jnp.broadcast_to(lse[part], (SUB, DH))


def in_vmem(n):
    return [pl.BlockSpec(memory_space=pltpu.VMEM)] * n


def suffix_partial(q, sk, sv, lengths):
    rows = q.shape[0]
    return pl.pallas_call(
        suffix_kernel,
        in_specs=[pl.BlockSpec(memory_space=pltpu.SMEM)] + in_vmem(3),
        out_specs=in_vmem(2),
        out_shape=[jax.ShapeDtypeStruct((GROUP * rows, DH), F32)] * 2,
        compiler_params=params(12),
        cost_estimate=cost(3.0),
    )(lengths, q, sk, sv)


def stack_kernel(pieces, a_ref, b_ref, o_ref, sems):
    rows = a_ref.shape[0]
    step = rows // pieces
    copies = []
    for i, ref in enumerate((a_ref, b_ref)):
        for j in range(pieces):
            n = i * pieces + j
            copies.append(
                pltpu.make_async_copy(
                    ref.at[pl.ds(j * step, step)], o_ref.at[pl.ds(n * step, step)], sems.at[n]
                )
            )
    for copy in copies:
        copy.start()
    for copy in copies:
        copy.wait()


def stacked(a, b, pieces, mib):
    rows, width = a.shape
    return pl.pallas_call(
        functools.partial(stack_kernel, pieces),
        in_specs=[pl.BlockSpec(memory_space=pl.ANY)] * 2,
        out_specs=pl.BlockSpec(memory_space=pltpu.VMEM),
        out_shape=jax.ShapeDtypeStruct((2 * rows, width), a.dtype),
        scratch_shapes=[pltpu.SemaphoreType.DMA((2 * pieces,))],
        compiler_params=params(mib),
        cost_estimate=cost(0.8),
    )(a, b)


TILE = 16


def spread(part):
    rows = (part.shape[0] - TILE) // GROUP
    strip = part[GROUP * rows :, :].astype(F32)
    lane = lax.broadcasted_iota(jnp.int32, (TILE, DH), 1)
    row = lax.broadcasted_iota(jnp.int32, (DH, WIDTH), 0)
    head = lax.shift_right_logical(
        lax.broadcasted_iota(jnp.int32, (DH, WIDTH), 1), DH.bit_length() - 1
    )
    chosen = jnp.zeros((DH, WIDTH), F32)
    pieces = []
    for n in range(rows // TILE):
        first = 3 * GROUP * n
        mine = (lane >= first) & (lane < first + 3 * GROUP)
        pieces.append(jnp.where(mine, strip, 0.0))
        at = first + 3 * head
        chosen = jnp.where((row >= at) & (row < at + 3), 1.0, chosen)
    pieces = jnp.concatenate(pieces, axis=0).astype(BF16)
    return heads_of(jnp.dot(pieces, chosen.astype(BF16), preferred_element_type=F32))


def pack(o_ref, first, values, logs):
    many = values.shape[0]
    rows = many // GROUP
    o_ref[first : first + many, :] = values.astype(BF16)
    lane = lax.broadcasted_iota(jnp.int32, (TILE, DH), 1)
    strip = jnp.zeros((TILE, DH), F32)
    for n in range(rows // TILE):
        for h in range(GROUP):
            rest = logs[h * rows + n * TILE : h * rows + (n + 1) * TILE]
            for j in range(3):
                piece = rest.astype(BF16).astype(F32)
                rest = rest - piece
                strip = jnp.where(lane == 3 * (n * GROUP + h) + j, piece, strip)
    o_ref[first + many : first + many + TILE, :] = strip.astype(BF16)


def locate(counts, at):
    for i, count in enumerate(counts):
        if at < count:
            return i, at
        at -= count


def prefix_kernel(groups, half, blocks, olds, joins, packed, skip, *refs):
    refs = list(refs)

    def take(n):
        return [refs.pop(0) for _ in range(n)]

    qs, kvs = take(groups), take(blocks)
    old_refs, part_refs = take(2 * len(olds)), take(len(joins))
    rows = qs[0].shape[0] // 2
    size = kvs[0].shape[0] // 2
    many = GROUP * rows

    def scores(g, b):
        q = heads_of(qs[g][half * rows : (half + 1) * rows, :])
        return lax.dot_general(
            q, kvs[b][:size, :], (((1,), (1,)), ((), ())), preferred_element_type=F32
        )

    units = [(g, b) for g in range(groups) for b in range(blocks)]
    ahead = scores(*units[0])
    for at, (g, b) in enumerate(units):
        s = ahead
        if at + 1 < len(units):
            ahead = scores(*units[at + 1])
        if b == 0:
            peak = None
            if olds:
                i, n = locate(olds, skip + g)
                span = slice(n * many, (n + 1) * many)
                both = old_refs[2 * i][span, :]
                peak = old_refs[2 * i + 1][span, 0:1]
        top = jnp.max(s, axis=1, keepdims=True) * SCALE2
        new = top if peak is None else jnp.maximum(peak, top)
        p = jnp.exp2(s * SCALE2 - new).astype(BF16)
        v = kvs[b][size:, :]
        added = jnp.dot(
            p, jnp.concatenate([v, jnp.ones_like(v)], axis=1), preferred_element_type=F32
        )
        both = added if peak is None else both * jnp.exp2(peak - new) + added
        peak = new
        if b < blocks - 1:
            continue
        level = jnp.broadcast_to(peak, (many, DH))
        if not packed:
            span = slice(g * many, (g + 1) * many)
            refs[0][span, :] = both
            refs[1][span, :] = level
            continue
        acc, total = both[:, :DH], both[:, DH:]
        if joins:
            i, n = locate(joins, skip + g)
            part = part_refs[i][n * (many + TILE) : (n + 1) * (many + TILE), :]
            logs = spread(part)
            new = jnp.maximum(level, logs)
            fade, weight = jnp.exp2(level - new), jnp.exp2(logs - new)
            acc = acc * fade + part[:many, :].astype(F32) * weight
            total = total * fade + weight
            level = new
        o_ref, first = (refs[0], g * (many + TILE)) if packed == "one" else (refs[g], 0)
        pack(o_ref, first, acc / total, level + jnp.log2(total))


def prefix_partial(queries, half, blocks, olds=(), joins=(), packed=None, skip=0):
    rows = queries[0].shape[0] // 2
    groups = len(queries)
    many = GROUP * rows
    keys = sum(b.shape[0] // 2 for b in blocks)
    arrays = [*queries, *blocks, *(a for old in olds for a in old), *joins]
    if packed == "one":
        outs = [jax.ShapeDtypeStruct((groups * (many + TILE), DH), BF16)]
    elif packed:
        outs = [jax.ShapeDtypeStruct((many + TILE, DH), BF16)] * groups
    else:
        outs = [jax.ShapeDtypeStruct((groups * many, n * DH), F32) for n in (2, 1)]
    kernel = functools.partial(
        prefix_kernel,
        groups,
        half,
        len(blocks),
        [old[0].shape[0] // many for old in olds],
        [part.shape[0] // (many + TILE) for part in joins],
        packed,
        skip,
    )
    return pl.pallas_call(
        kernel,
        in_specs=in_vmem(len(arrays)),
        out_specs=in_vmem(len(outs)),
        out_shape=outs,
        compiler_params=params(16),
        cost_estimate=cost(0.5 + 1.4e-6 * groups * many * keys),
    )(*arrays)


def merged(parts, mixed, lse):
    logs = [lse] + [spread(part) for part in parts]
    many = mixed.shape[0]
    rows = many // GROUP
    values = [mixed] + [part[:many, :].astype(F32) for part in parts]
    peak = functools.reduce(jnp.maximum, logs)
    weights = [jnp.exp2(log - peak) for log in logs]
    total = functools.reduce(jnp.add, weights)
    value = functools.reduce(jnp.add, [w * o for w, o in zip(weights, values)])
    value = (value / total).astype(BF16)
    return jnp.concatenate([value[h * rows : (h + 1) * rows] for h in range(GROUP)], axis=1)


def project_kernel(first, merge, index_ref, weight_ref, *refs):
    refs = list(refs)
    piece = weight_ref.shape[1] // (NH * NY)
    if merge:
        *parts, mixed, lse = refs[: NZ + 2]
        *outs, att_ref = refs[NZ + 2 :]
        att = merged([p[...] for p in parts], mixed[...], lse[...])
        att_ref[...] = att
    else:
        att = refs[0][...]
        outs = refs[1:]
    for k, o in enumerate(outs):
        at = pl.multiple_of(index_ref[first + k] * piece, piece)
        w = weight_ref[:, pl.ds(at, piece)]
        o[...] = jnp.dot(att, w, preferred_element_type=F32).astype(o.dtype)


def project(rows, index, first, inputs, weight, merge):
    depth, columns = weight.shape
    piece = columns // (NH * NY)
    outs = [jax.ShapeDtypeStruct((rows, piece), F32 if k == 0 else BF16) for k in range(NY)]
    if merge:
        outs.append(jax.ShapeDtypeStruct((rows, depth), BF16))
    return pl.pallas_call(
        functools.partial(project_kernel, first, merge),
        in_specs=[pl.BlockSpec(memory_space=pltpu.SMEM)] + in_vmem(1 + len(inputs)),
        out_specs=in_vmem(len(outs)),
        out_shape=outs,
        compiler_params=params(16),
        cost_estimate=cost(3.0),
    )(index, weight, *inputs)


def on_device(
    queries, prefix_keys, prefix_values, suffix_keys, suffix_values, suffix_lengths, out_weight
):
    here = lax.axis_index("tensor").astype(jnp.int32)
    step = jnp.arange(NH * NY, dtype=jnp.int32)
    index = (here + NY * (1 - step // NY)) // NY % NH * NY + (here + step) % NY

    send = functools.partial(lax.ppermute, axis_name="blk")
    far_queries = send(queries, perm=blk_perm(dx=2))
    own = stacked(prefix_keys, prefix_values, 4, 56)
    peer = send(own, perm=blk_perm(dc=1))
    near = [send(own, perm=blk_perm(dx=d)) for d in (1, 3)]
    pair = stacked(queries, far_queries, 1, 4)
    shifts = (0, 3, 1, 2)
    group = [pair] + [send(pair, perm=blk_perm(dz=d)) for d in shifts[1:]]

    together = lax.optimization_barrier
    mixed, lse = suffix_partial(queries, suffix_keys, suffix_values, suffix_lengths)
    peer, index, lse = together((peer, index, lse))
    chip = [own, peer]
    (part_a,) = prefix_partial(group[:2], 1, chip, packed="one")
    part_a = send(part_a, perm=blk_perm(dx=2))
    state_a = prefix_partial(group[:2], 0, chip)
    rest, state_a = together((group[2:], state_a))
    group = group[:2] + rest
    (part_b,) = prefix_partial(rest, 1, chip, packed="one")
    near, part_b = together((near, part_b))
    part_b = send(part_b, perm=blk_perm(dx=2))
    near_peer = [send(b, perm=blk_perm(dc=1)) for b in near]
    state_b = prefix_partial(rest, 0, chip)
    state = prefix_partial(group, 0, near, [state_a, state_b])
    near_peer, state = together((near_peer, state))
    joins = [part_a, part_b]
    (third,) = prefix_partial(group[3:], 0, near_peer, [state], joins, "each", 3)
    state, third = together((state, third))
    away = prefix_partial(group[1:3], 0, near_peer, [state], joins, "each", 1)
    state, away = together((state, away))
    away = [send(part, perm=blk_perm(dz=-d)) for d, part in zip((2, 3, 1), [third, *away])]
    home = prefix_partial(group[:1], 0, near_peer, [state], joins, "each")
    parts = [*home, *away]

    send = functools.partial(lax.ppermute, axis_name="tensor")
    *away, attention = project(queries.shape[0], index, 0, parts + [mixed, lse], out_weight, True)
    away = [away[0]] + [send(away[d], perm=tensor_perm(dy=d)) for d in (1, 2, 3)]
    home = project(queries.shape[0], index, NY, [attention], out_weight, False)
    home = [home[0]] + [send(home[d], perm=tensor_perm(dy=d)) for d in (1, 2, 3)]

    def summed(pieces):
        return functools.reduce(jnp.add, [p.astype(F32) for p in pieces])

    other = send(summed(away).astype(BF16), perm=tensor_perm(dh=1))
    return summed(home + [other]).astype(BF16)


def solution(mesh):
    in_specs = (
        P("blk", "tensor"),
        P("blk", "tensor"),
        P("blk", "tensor"),
        P("blk", None, "tensor"),
        P("blk", None, "tensor"),
        P("blk"),
        P("tensor", None),
    )
    out_specs = P("blk", "tensor")
    return jax.shard_map(
        on_device, mesh=mesh, in_specs=in_specs, out_specs=out_specs, check_vma=False
    )
```
